32 devices in a mesh: feat: 8 (over z, x), blk: 4 (over y, core).
Axes of the slice: x: 2, y: 2, z: 4, core: 2. Of those that a mesh axis runs over, the one named last changes fastest.
Arguments:
- features: bfloat16 [1024, 8, 4096], P('feat', None, 'blk'), may hold values from -6 to 6
- adj_local: bfloat16 [32768, 1024], P(('feat', 'blk')), may hold values from 0.049804688 to 1
- adj_remote: bfloat16 [32768, 768], P(('feat', 'blk')), may hold values from 0.049804688 to 1
- tile_mask: int32 [256, 14], P(('feat', 'blk')), may hold values from 0 to 1, as said below
- w_self: bfloat16 [1024, 256], replicated, may hold values from -0.1875 to 0.1875
- w_neigh: bfloat16 [1024, 256], replicated, may hold values from -0.1875 to 0.1875
- out_bias: float32 [256], replicated, may hold values from -4 to 4
Outputs:
- hidden_out: bfloat16 [32768, 256], P(('feat', 'blk'))
The draws below stay inside these ranges and needn't reach their ends.
Inputs may be any that keep to these rules, and one draw needn't show every extreme that they name: `tile_mask`: 0 or 1 for each tile; the 128 x 128 tiles on the diagonal of every node's adj_local block are 1.
All inputs are finite; a program needn't handle non-finite values.
Results may differ from the reference program's by a relative error of at most 0.0035.
Values may be sent and summed in bfloat16 or wider, within the bound.
A program may use at most 128 MiB of HBM per device.

```python
import jax
import jax.numpy as jnp
from jax import lax

F = 1024
HID = 256
TILE = 128
NB = 1024
HALO = 256
NODES = 32768
N_FEAT = 8
N_BLK = 4


def draw_tile_mask(key, part):
    tile_rows = NODES // TILE
    tile_cols = (NB + (N_BLK - 1) * HALO) // TILE
    per_device = NB // TILE
    device_count = tile_rows // per_device
    key_level = jax.random.fold_in(key, 11)
    key_tiles = jax.random.fold_in(key, 23)
    dense_device = jax.random.randint(key_level, (device_count,), 0, 4) == 0
    density = jnp.where(dense_device, 16, 1)
    density_rows = jnp.repeat(density, per_device)
    uniform_level = jax.random.randint(key_tiles, (tile_rows, tile_cols), 0, 16)
    alive_tile = uniform_level < density_rows[:, None]
    row_pos = jnp.arange(tile_rows) % per_device
    col_pos = jnp.arange(tile_cols)
    on_diagonal = row_pos[:, None] == col_pos[None, :]
    return jnp.where(alive_tile | on_diagonal, 1, 0).astype(jnp.int32)


def levels(stream_key, dims, shards, smallest, top_value):
    level = 1.0
    for dim, shards_of in shards:
        heights = jax.random.uniform(jax.random.fold_in(jax.random.fold_in(stream_key, 6), dim), (shards_of,), jnp.float32, smallest / len(shards), top_value / len(shards))
        level = level * jnp.repeat(jnp.exp(heights), dims[dim] // shards_of).reshape((-1,) + (1,) * (len(dims) - 1 - dim))
    return level


def noise(stream_key, dims, spread, most, shards=(), kind=jnp.bfloat16):
    array = jax.random.normal(stream_key, dims, jnp.float32) * spread
    if len(shards) > 0:
        array = levels(stream_key, dims, shards, -0.22, 0.18) * array
    return jnp.clip(array, min=-most, max=most).astype(kind)


def setup_inputs(seed: int = 0) -> dict:
    splits = jax.random.split(jax.random.key(seed), 8)
    features = noise(splits[0], (F, N_FEAT, N_BLK * NB), 1.0, 6.0, ((0, 8), (2, 4)))
    adj_local = jnp.clip(0.049804688 + 0.9501953 * jax.random.uniform(splits[1], (NODES, NB), jnp.float32) ** levels(splits[1], (NODES, NB), ((0, 32),), -0.2, 0.2), 0.049804688, 1.0).astype(jnp.bfloat16)
    adj_remote = jnp.clip(0.049804688 + 0.9501953 * jax.random.uniform(splits[2], (NODES, (N_BLK - 1) * HALO), jnp.float32) ** levels(splits[2], (NODES, (N_BLK - 1) * HALO), ((0, 32),), -0.2, 0.2), 0.049804688, 1.0).astype(jnp.bfloat16)
    tile_mask = draw_tile_mask(jax.random.fold_in(splits[7], 71), 0)
    w_self = noise(splits[4], (F, HID), F ** -0.5, 0.1875)
    w_neigh = noise(splits[5], (F, HID), F ** -0.5, 0.1875)
    out_bias = noise(splits[6], (HID,), 1.0, 4.0, (), jnp.float32)
    return dict(features=features, adj_local=adj_local, adj_remote=adj_remote, tile_mask=tile_mask, w_self=w_self, w_neigh=w_neigh, out_bias=out_bias)


def expand_tiles(adjacency, tile_flags):
    row_total, col_total = adjacency.shape
    blocked = adjacency.reshape(row_total // TILE, TILE, col_total // TILE, TILE)
    blocked = blocked * tile_flags.astype(jnp.bfloat16)[:, None, :, None]
    return blocked.reshape(row_total, col_total)

def reference(features, adj_local, adj_remote, tile_mask, w_self, w_neigh, out_bias):
    local_tiles = NB // TILE
    zero_index = jnp.zeros((), jnp.int32)
    wide_neigh = w_neigh.astype(jnp.float32)

    def one_block(block_id):
        group_id = (block_id // N_BLK).astype(jnp.int32)
        block_pos = (block_id % N_BLK).astype(jnp.int32)
        own_feats = lax.dynamic_slice(features, (zero_index, group_id, (block_pos * NB).astype(jnp.int32)), (F, 1, NB)).reshape(F, NB)
        row_start = (block_id * NB).astype(jnp.int32)
        tile_start = (block_id * local_tiles).astype(jnp.int32)
        tile_flags = lax.dynamic_slice_in_dim(tile_mask, tile_start, local_tiles, 0)
        live_local = expand_tiles(lax.dynamic_slice_in_dim(adj_local, row_start, NB, 0), tile_flags[:, :local_tiles])
        live_remote = expand_tiles(lax.dynamic_slice_in_dim(adj_remote, row_start, NB, 0), tile_flags[:, local_tiles:])
        degree = lax.optimization_barrier(jnp.sum(live_local.astype(jnp.float32), axis=1)) + lax.optimization_barrier(jnp.sum(live_remote.astype(jnp.float32), axis=1))
        summed = jnp.dot(live_local, own_feats.T, preferred_element_type=jnp.float32)
        for offset in range(1, N_BLK):
            source = ((block_pos + (N_BLK - offset)) % N_BLK).astype(jnp.int32)
            halo_panel = lax.dynamic_slice(features, (zero_index, group_id, (source * NB).astype(jnp.int32)), (F, 1, HALO)).reshape(F, HALO)
            weight_piece = live_remote[:, (offset - 1) * HALO:offset * HALO]
            summed = summed + jnp.dot(weight_piece, halo_panel.T, preferred_element_type=jnp.float32)
        neigh_term = jnp.dot(summed, wide_neigh, precision=lax.Precision.HIGHEST) / jnp.sqrt(degree)[:, None]
        self_term = jnp.dot(own_feats.T, w_self, preferred_element_type=jnp.float32)
        return jax.nn.relu(self_term + neigh_term + out_bias[None, :]).astype(jnp.bfloat16)
    blocks = lax.map(one_block, jnp.arange(N_FEAT * N_BLK, dtype=jnp.int32))
    return blocks.reshape(NODES, HID)
```

```python
import functools

import jax
import jax.numpy as jnp
from jax import lax
from jax.experimental import pallas as pl
from jax.experimental.pallas import tpu as pltpu
from jax.sharding import PartitionSpec as P

TILE = 128
CHUNK = 128
MESH = pl.DeviceIdType.MESH


def far_first(count):
    return sorted(range(1, count), key=lambda d: abs(2 * d - count))


def layer_kernel(
    parts, blocks,
    features, adj_local, adj_remote, tile_mask, w_self, w_neigh, out_bias, out,
    loaded, spread, outgoing, own, live, mask, weights, bias,
    projected, halo, self_bias, total, inverse,
    load_sem, misc_sem, send_sem, recv_sem, halo_send, halo_recv,
):
    width = features.shape[0]
    nodes = features.shape[2]
    hidden = w_self.shape[1]
    remote = adj_remote.shape[1]
    halo_len = remote // (blocks - 1)
    chunks = nodes // CHUNK
    halo_chunks = halo_len // CHUNK
    row_tiles = nodes // TILE
    local_tiles = nodes // TILE
    col_tiles = local_tiles + remote // TILE
    me = lax.axis_index("feat")
    my_block = lax.axis_index("blk")
    peers = [lax.rem(me + d, parts) for d in far_first(parts)]
    block_peers = [lax.rem(my_block + k, blocks) for k in range(1, blocks)]

    barrier = pltpu.get_barrier_semaphore()
    for peer in peers:
        pl.semaphore_signal(barrier, inc=1, device_id={"feat": peer}, device_id_type=MESH)
    for peer in block_peers:
        pl.semaphore_signal(barrier, inc=1, device_id={"blk": peer}, device_id_type=MESH)

    def load(k):
        columns = pl.ds(pl.multiple_of(k * CHUNK, CHUNK), CHUNK)
        return pltpu.make_async_copy(features.at[:, :, columns], loaded.at[k], load_sem.at[k])

    others = [
        pltpu.make_async_copy(tile_mask, mask, misc_sem.at[0]),
        pltpu.make_async_copy(out_bias, bias, misc_sem.at[1]),
        pltpu.make_async_copy(w_self, weights.at[:, pl.ds(0, hidden)], misc_sem.at[2]),
        pltpu.make_async_copy(w_neigh, weights.at[:, pl.ds(hidden, hidden)], misc_sem.at[3]),
        pltpu.make_async_copy(adj_local, live.at[:, pl.ds(0, nodes)], misc_sem.at[4]),
        pltpu.make_async_copy(adj_remote, live.at[:, pl.ds(nodes, remote)], misc_sem.at[5]),
    ]
    for k in range(chunks):
        load(k).start()
    for copy in others:
        copy.start()

    def rows_of(part):
        return pl.ds(pl.multiple_of(part * width, width), width)

    def send(k, peer):
        return pltpu.make_async_remote_copy(
            src_ref=outgoing.at[k, peer],
            dst_ref=own.at[k, rows_of(me)],
            send_sem=send_sem.at[k, peer],
            recv_sem=recv_sem.at[k, me],
            device_id={"feat": peer},
            device_id_type=MESH,
        )

    def arrival(k, peer):
        return pltpu.make_async_remote_copy(
            src_ref=outgoing.at[k, peer],
            dst_ref=own.at[k, rows_of(peer)],
            send_sem=send_sem.at[k, peer],
            recv_sem=recv_sem.at[k, peer],
            device_id={"feat": peer},
            device_id_type=MESH,
        )

    def regroup(k):
        load(k).wait()
        spread[...] = loaded[k].astype(jnp.float32).reshape(width * parts, CHUNK)
        for g in range(parts):
            outgoing[k, g] = spread[pl.ds(g, width, stride=parts), :].astype(jnp.bfloat16)

    def dispatch(k):
        for peer in peers:
            send(k, peer).start()
        own[k, rows_of(me)] = outgoing[k, me]

    regroup(0)
    pl.semaphore_wait(barrier, parts - 1 + blocks - 1)
    dispatch(0)

    @pl.loop(1, chunks)
    def _(k):
        regroup(k)
        dispatch(k)

    for copy in others:
        copy.wait()

    @pl.loop(0, row_tiles)
    def _(i):
        rows = pl.ds(pl.multiple_of(i * TILE, TILE), TILE)
        sums = jnp.zeros((TILE, TILE), jnp.float32)
        for j in range(col_tiles):
            columns = pl.ds(j * TILE, TILE)
            piece = live[rows, columns].astype(jnp.float32) * mask[i, j].astype(jnp.float32)
            live[rows, columns] = piece.astype(jnp.bfloat16)
            sums = sums + piece
        degree = jnp.sum(sums, axis=1, keepdims=True)
        inverse[rows, :] = jnp.broadcast_to(1.0 / jnp.sqrt(degree), (TILE, TILE))
        total[rows, :] = jnp.zeros((TILE, hidden), jnp.float32)

    bias_row = bias[...].reshape(1, hidden)

    def project(k):
        for peer in peers:
            arrival(k, peer).wait_recv()
        both = lax.dot_general(
            own[k], weights[...], (((0,), (0,)), ((), ())), preferred_element_type=jnp.float32
        )
        rows = pl.ds(pl.multiple_of(k * CHUNK, CHUNK), CHUNK)
        self_bias[rows, :] = both[:, :hidden] + bias_row
        projected[rows, :] = both[:, hidden:].astype(jnp.bfloat16)

    def add_local(k):
        span = pl.ds(pl.multiple_of(k * CHUNK, CHUNK), CHUNK)
        panel = projected[span, :]

        @pl.loop(0, row_tiles)
        def _(i):
            rows = pl.ds(pl.multiple_of(i * TILE, TILE), TILE)
            total[rows, :] += jnp.dot(live[rows, span], panel, preferred_element_type=jnp.float32)

    def halo_copy(slot, peer):
        return pltpu.make_async_remote_copy(
            src_ref=projected.at[pl.ds(0, halo_len)],
            dst_ref=halo.at[pl.ds(slot * halo_len, halo_len)],
            send_sem=halo_send.at[slot],
            recv_sem=halo_recv.at[slot],
            device_id={"blk": peer},
            device_id_type=MESH,
        )

    @pl.loop(0, halo_chunks)
    def _(k):
        project(k)

    for slot, peer in enumerate(block_peers):
        halo_copy(slot, peer).start()

    @pl.loop(0, halo_chunks)
    def _(k):
        add_local(k)

    for slot, peer in enumerate(block_peers):
        halo_copy(slot, peer).wait()

    @pl.loop(0, row_tiles)
    def _(i):
        rows = pl.ds(pl.multiple_of(i * TILE, TILE), TILE)
        total[rows, :] += jnp.dot(
            live[rows, pl.ds(nodes, remote)], halo[...], preferred_element_type=jnp.float32
        )

    @pl.loop(halo_chunks, chunks - 1)
    def _(k):
        project(k)
        add_local(k)

    last = chunks - 1
    project(last)
    span = pl.ds(last * CHUNK, CHUNK)
    panel = projected[span, :]

    @pl.loop(0, row_tiles)
    def _(i):
        rows = pl.ds(pl.multiple_of(i * TILE, TILE), TILE)
        summed = total[rows, :] + jnp.dot(
            live[rows, span], panel, preferred_element_type=jnp.float32
        )
        scale = jnp.concatenate([inverse[rows, :]] * (hidden // TILE), axis=1)
        out[rows, :] = jnp.maximum(self_bias[rows, :] + summed * scale, 0.0).astype(jnp.bfloat16)

    @pl.loop(0, chunks)
    def _(k):
        for peer in peers:
            arrival(k, peer).wait_send()


def shards(features, adj_local, adj_remote, tile_mask, w_self, w_neigh, out_bias):
    parts = lax.axis_size("feat")
    blocks = lax.axis_size("blk")
    width, _, nodes = features.shape
    hidden = w_self.shape[1]
    remote = adj_remote.shape[1]
    chunks = nodes // CHUNK
    bf16, f32 = jnp.bfloat16, jnp.float32
    hbm = pl.BlockSpec(memory_space=pltpu.HBM)
    return pl.pallas_call(
        functools.partial(layer_kernel, parts, blocks),
        out_shape=jax.ShapeDtypeStruct((nodes, hidden), bf16),
        in_specs=[hbm] * 7,
        out_specs=pl.BlockSpec(memory_space=pltpu.VMEM),
        scratch_shapes=[
            pltpu.VMEM((chunks, width, parts, CHUNK), bf16),
            pltpu.VMEM((width * parts, CHUNK), f32),
            pltpu.VMEM((chunks, parts, width, CHUNK), bf16),
            pltpu.VMEM((chunks, parts * width, CHUNK), bf16),
            pltpu.VMEM((nodes, nodes + remote), bf16),
            pltpu.SMEM(tile_mask.shape, jnp.int32),
            pltpu.VMEM((parts * width, 2 * hidden), bf16),
            pltpu.VMEM(out_bias.shape, f32),
            pltpu.VMEM((nodes, hidden), bf16),
            pltpu.VMEM((remote, hidden), bf16),
            pltpu.VMEM((nodes, hidden), f32),
            pltpu.VMEM((nodes, hidden), f32),
            pltpu.VMEM((nodes, TILE), f32),
            pltpu.SemaphoreType.DMA((chunks,)),
            pltpu.SemaphoreType.DMA((6,)),
            pltpu.SemaphoreType.DMA((chunks, parts)),
            pltpu.SemaphoreType.DMA((chunks, parts)),
            pltpu.SemaphoreType.DMA((blocks - 1,)),
            pltpu.SemaphoreType.DMA((blocks - 1,)),
        ],
        compiler_params=pltpu.CompilerParams(
            collective_id=0, has_side_effects=True, vmem_limit_bytes=62 * 1024 * 1024
        ),
    )(features, adj_local, adj_remote, tile_mask, w_self, w_neigh, out_bias)


def solution(mesh):
    placed = (
        P("feat", None, "blk"),
        P(("feat", "blk"), None),
        P(("feat", "blk"), None),
        P(("feat", "blk"), None),
        P(),
        P(),
        P(),
    )
    return jax.shard_map(
        shards, mesh=mesh, in_specs=placed, out_specs=P(("feat", "blk"), None), check_vma=False
    )
```

```python
import functools

import jax
import jax.numpy as jnp
from jax import lax
from jax.experimental import pallas as pl
from jax.experimental.pallas import tpu as pltpu
from jax.sharding import PartitionSpec as P

TILE = 128
CHUNK = 256
MESH = pl.DeviceIdType.MESH


def layer_kernel(
    parts, blocks,
    features, adj_local, adj_remote, tile_mask, w_self, w_neigh, out_bias, out,
    loaded, spread, outgoing, own, live, mask, weights, bias,
    projected, halo, self_bias, total, inverse,
    load_sem, misc_sem, send_sem, recv_sem, halo_send, halo_recv,
):
    width = features.shape[0]
    nodes = features.shape[2]
    hidden = w_self.shape[1]
    remote = adj_remote.shape[1]
    halo_len = remote // (blocks - 1)
    chunks = nodes // CHUNK
    halo_chunks = halo_len // CHUNK
    row_tiles = nodes // TILE
    local_tiles = nodes // TILE
    col_tiles = local_tiles + remote // TILE
    me = lax.axis_index("feat")
    my_block = lax.axis_index("blk")
    peers = [lax.rem(me + d, parts) for d in range(1, parts)]
    block_peers = [lax.rem(my_block + k, blocks) for k in range(1, blocks)]

    barrier = pltpu.get_barrier_semaphore()
    for peer in peers:
        pl.semaphore_signal(barrier, inc=1, device_id={"feat": peer}, device_id_type=MESH)
    for peer in block_peers:
        pl.semaphore_signal(barrier, inc=1, device_id={"blk": peer}, device_id_type=MESH)

    def load(k):
        columns = pl.ds(pl.multiple_of(k * CHUNK, CHUNK), CHUNK)
        return pltpu.make_async_copy(features.at[:, :, columns], loaded.at[k], load_sem.at[k])

    others = [
        pltpu.make_async_copy(tile_mask, mask, misc_sem.at[0]),
        pltpu.make_async_copy(out_bias, bias, misc_sem.at[1]),
        pltpu.make_async_copy(w_self, weights.at[:, pl.ds(0, hidden)], misc_sem.at[2]),
        pltpu.make_async_copy(w_neigh, weights.at[:, pl.ds(hidden, hidden)], misc_sem.at[3]),
        pltpu.make_async_copy(adj_local, live.at[:, pl.ds(0, nodes)], misc_sem.at[4]),
        pltpu.make_async_copy(adj_remote, live.at[:, pl.ds(nodes, remote)], misc_sem.at[5]),
    ]
    for k in range(chunks):
        load(k).start()
    for copy in others:
        copy.start()

    def rows_of(part):
        return pl.ds(pl.multiple_of(part * width, width), width)

    def send(k, peer):
        return pltpu.make_async_remote_copy(
            src_ref=outgoing.at[k, peer],
            dst_ref=own.at[k, rows_of(me)],
            send_sem=send_sem.at[k, peer],
            recv_sem=recv_sem.at[k, me],
            device_id={"feat": peer},
            device_id_type=MESH,
        )

    def arrival(k, peer):
        return pltpu.make_async_remote_copy(
            src_ref=outgoing.at[k, peer],
            dst_ref=own.at[k, rows_of(peer)],
            send_sem=send_sem.at[k, peer],
            recv_sem=recv_sem.at[k, peer],
            device_id={"feat": peer},
            device_id_type=MESH,
        )

    def regroup(k):
        load(k).wait()
        for t in range(CHUNK // TILE):
            lanes = pl.ds(t * TILE, TILE)
            spread[t] = loaded[k, :, :, lanes].astype(jnp.float32).reshape(width * parts, TILE)
            for g in range(parts):
                piece = spread[t, pl.ds(g, width, stride=parts), :]
                outgoing[k, g, :, lanes] = piece.astype(jnp.bfloat16)

    def dispatch(k):
        for peer in peers:
            send(k, peer).start()
        own[k, rows_of(me)] = outgoing[k, me]

    regroup(0)
    pl.semaphore_wait(barrier, parts - 1 + blocks - 1)
    dispatch(0)

    @pl.loop(1, chunks)
    def _(k):
        regroup(k)
        dispatch(k)

    for copy in others:
        copy.wait()

    @pl.loop(0, row_tiles)
    def _(i):
        rows = pl.ds(pl.multiple_of(i * TILE, TILE), TILE)
        sums = jnp.zeros((TILE, TILE), jnp.float32)
        for j in range(col_tiles):
            columns = pl.ds(j * TILE, TILE)
            piece = live[rows, columns].astype(jnp.float32) * mask[i, j].astype(jnp.float32)
            live[rows, columns] = piece.astype(jnp.bfloat16)
            sums = sums + piece
        degree = jnp.sum(sums, axis=1, keepdims=True)
        inverse[rows, :] = jnp.broadcast_to(1.0 / jnp.sqrt(degree), (TILE, TILE))
        total[rows, :] = jnp.zeros((TILE, hidden), jnp.float32)

    bias_row = bias[...].reshape(1, hidden)

    def project(k):
        for peer in peers:
            arrival(k, peer).wait_recv()
        both = lax.dot_general(
            own[k], weights[...], (((0,), (0,)), ((), ())), preferred_element_type=jnp.float32
        )
        rows = pl.ds(pl.multiple_of(k * CHUNK, CHUNK), CHUNK)
        self_bias[rows, :] = both[:, :hidden] + bias_row
        projected[rows, :] = both[:, hidden:].astype(jnp.bfloat16)

    def sent(k):
        for peer in peers:
            arrival(k, peer).wait_send()

    def add_local(k):
        span = pl.ds(pl.multiple_of(k * CHUNK, CHUNK), CHUNK)
        panel = projected[span, :]

        @pl.loop(0, row_tiles)
        def _(i):
            rows = pl.ds(pl.multiple_of(i * TILE, TILE), TILE)
            total[rows, :] += jnp.dot(live[rows, span], panel, preferred_element_type=jnp.float32)

    def halo_copy(slot, peer):
        return pltpu.make_async_remote_copy(
            src_ref=projected.at[pl.ds(0, halo_len)],
            dst_ref=halo.at[pl.ds(slot * halo_len, halo_len)],
            send_sem=halo_send.at[slot],
            recv_sem=halo_recv.at[slot],
            device_id={"blk": peer},
            device_id_type=MESH,
        )

    @pl.loop(0, halo_chunks)
    def _(k):
        project(k)

    for slot, peer in enumerate(block_peers):
        halo_copy(slot, peer).start()

    @pl.loop(0, halo_chunks)
    def _(k):
        add_local(k)
        sent(k)

    for slot, peer in enumerate(block_peers):
        halo_copy(slot, peer).wait()

    @pl.loop(0, row_tiles)
    def _(i):
        rows = pl.ds(pl.multiple_of(i * TILE, TILE), TILE)
        total[rows, :] += jnp.dot(
            live[rows, pl.ds(nodes, remote)], halo[...], preferred_element_type=jnp.float32
        )

    @pl.loop(halo_chunks, chunks - 1)
    def _(k):
        project(k)
        add_local(k)
        sent(k)

    last = chunks - 1
    project(last)
    span = pl.ds(last * CHUNK, CHUNK)
    panel = projected[span, :]

    @pl.loop(0, row_tiles)
    def _(i):
        rows = pl.ds(pl.multiple_of(i * TILE, TILE), TILE)
        summed = total[rows, :] + jnp.dot(
            live[rows, span], panel, preferred_element_type=jnp.float32
        )
        scale = jnp.concatenate([inverse[rows, :]] * (hidden // TILE), axis=1)
        out[rows, :] = jnp.maximum(self_bias[rows, :] + summed * scale, 0.0).astype(jnp.bfloat16)

    sent(last)


def shards(features, adj_local, adj_remote, tile_mask, w_self, w_neigh, out_bias):
    parts = lax.axis_size("feat")
    blocks = lax.axis_size("blk")
    width, _, nodes = features.shape
    hidden = w_self.shape[1]
    remote = adj_remote.shape[1]
    chunks = nodes // CHUNK
    bf16, f32 = jnp.bfloat16, jnp.float32
    hbm = pl.BlockSpec(memory_space=pltpu.HBM)
    return pl.pallas_call(
        functools.partial(layer_kernel, parts, blocks),
        out_shape=pltpu.VMEM((nodes, hidden), bf16),
        in_specs=[hbm] * 7,
        out_specs=pl.BlockSpec(memory_space=pltpu.VMEM),
        scratch_shapes=[
            pltpu.VMEM((chunks, width, parts, CHUNK), bf16),
            pltpu.VMEM((CHUNK // TILE, width * parts, TILE), f32),
            pltpu.VMEM((chunks, parts, width, CHUNK), bf16),
            pltpu.VMEM((chunks, parts * width, CHUNK), bf16),
            pltpu.VMEM((nodes, nodes + remote), bf16),
            pltpu.SMEM(tile_mask.shape, jnp.int32),
            pltpu.VMEM((parts * width, 2 * hidden), bf16),
            pltpu.VMEM(out_bias.shape, f32),
            pltpu.VMEM((nodes, hidden), bf16),
            pltpu.VMEM((remote, hidden), bf16),
            pltpu.VMEM((nodes, hidden), f32),
            pltpu.VMEM((nodes, hidden), f32),
            pltpu.VMEM((nodes, TILE), f32),
            pltpu.SemaphoreType.DMA((chunks,)),
            pltpu.SemaphoreType.DMA((6,)),
            pltpu.SemaphoreType.DMA((chunks, parts)),
            pltpu.SemaphoreType.DMA((chunks, parts)),
            pltpu.SemaphoreType.DMA((blocks - 1,)),
            pltpu.SemaphoreType.DMA((blocks - 1,)),
        ],
        compiler_params=pltpu.CompilerParams(
            collective_id=0, has_side_effects=True, vmem_limit_bytes=62 * 1024 * 1024
        ),
    )(features, adj_local, adj_remote, tile_mask, w_self, w_neigh, out_bias)


def solution(mesh):
    placed = (
        P("feat", None, "blk"),
        P(("feat", "blk"), None),
        P(("feat", "blk"), None),
        P(("feat", "blk"), None),
        P(),
        P(),
        P(),
    )
    return jax.shard_map(
        shards, mesh=mesh, in_specs=placed, out_specs=P(("feat", "blk"), None), check_vma=False
    )
```

```python
import functools

import jax
import jax.numpy as jnp
from jax import lax
from jax.experimental import pallas as pl
from jax.experimental.pallas import tpu as pltpu
from jax.sharding import PartitionSpec as P

TILE = 128
CHUNK = 256
MESH = pl.DeviceIdType.MESH


def layer_kernel(
    parts, blocks,
    features, adj_local, adj_remote, tile_mask, w_self, w_neigh, out_bias, out,
    loaded, spread, outgoing, own, live, mask, weights, bias,
    projected, halo, self_bias, total, inverse,
    load_sem, misc_sem, send_sem, recv_sem, halo_send, halo_recv,
):
    width = features.shape[0]
    nodes = features.shape[2]
    hidden = w_self.shape[1]
    remote = adj_remote.shape[1]
    halo_len = remote // (blocks - 1)
    chunks = nodes // CHUNK
    halo_chunks = halo_len // CHUNK
    row_tiles = nodes // TILE
    local_tiles = nodes // TILE
    col_tiles = local_tiles + remote // TILE
    me = lax.axis_index("feat")
    my_block = lax.axis_index("blk")
    peers = [lax.rem(me + d, parts) for d in range(1, parts)]
    block_peers = [lax.rem(my_block + k, blocks) for k in range(1, blocks)]

    barrier = pltpu.get_barrier_semaphore()
    for peer in peers:
        pl.semaphore_signal(barrier, inc=1, device_id={"feat": peer}, device_id_type=MESH)
    for peer in block_peers:
        pl.semaphore_signal(barrier, inc=1, device_id={"blk": peer}, device_id_type=MESH)

    def load(k):
        columns = pl.ds(pl.multiple_of(k * CHUNK, CHUNK), CHUNK)
        return pltpu.make_async_copy(features.at[:, :, columns], loaded.at[k], load_sem.at[k])

    others = [
        pltpu.make_async_copy(tile_mask, mask, misc_sem.at[0]),
        pltpu.make_async_copy(out_bias, bias, misc_sem.at[1]),
        pltpu.make_async_copy(w_self, weights.at[:, pl.ds(0, hidden)], misc_sem.at[2]),
        pltpu.make_async_copy(w_neigh, weights.at[:, pl.ds(hidden, hidden)], misc_sem.at[3]),
        pltpu.make_async_copy(adj_local, live.at[:, pl.ds(0, nodes)], misc_sem.at[4]),
        pltpu.make_async_copy(adj_remote, live.at[:, pl.ds(nodes, remote)], misc_sem.at[5]),
    ]
    for k in range(chunks):
        load(k).start()
    for copy in others:
        copy.start()

    def rows_of(part):
        return pl.ds(pl.multiple_of(part * width, width), width)

    def send(k, peer):
        return pltpu.make_async_remote_copy(
            src_ref=outgoing.at[k, peer],
            dst_ref=own.at[k, rows_of(me)],
            send_sem=send_sem.at[k, peer],
            recv_sem=recv_sem.at[k, me],
            device_id={"feat": peer},
            device_id_type=MESH,
        )

    def arrival(k, peer):
        return pltpu.make_async_remote_copy(
            src_ref=outgoing.at[k, peer],
            dst_ref=own.at[k, rows_of(peer)],
            send_sem=send_sem.at[k, peer],
            recv_sem=recv_sem.at[k, peer],
            device_id={"feat": peer},
            device_id_type=MESH,
        )

    def regroup(k):
        load(k).wait()
        for t in range(CHUNK // TILE):
            lanes = pl.ds(t * TILE, TILE)
            spread[t] = loaded[k, :, :, lanes].astype(jnp.float32).reshape(width * parts, TILE)
            for g in range(parts):
                piece = spread[t, pl.ds(g, width, stride=parts), :]
                outgoing[k, g, :, lanes] = piece.astype(jnp.bfloat16)

    def dispatch(k):
        for peer in peers:
            send(k, peer).start()
        own[k, rows_of(me)] = outgoing[k, me]

    regroup(0)
    pl.semaphore_wait(barrier, parts - 1 + blocks - 1)
    dispatch(0)

    @pl.loop(1, chunks)
    def _(k):
        regroup(k)
        dispatch(k)

    for copy in others:
        copy.wait()

    @pl.loop(0, row_tiles)
    def _(i):
        rows = pl.ds(pl.multiple_of(i * TILE, TILE), TILE)
        sums = jnp.zeros((TILE, TILE), jnp.float32)
        for j in range(col_tiles):
            columns = pl.ds(j * TILE, TILE)
            piece = live[rows, columns].astype(jnp.float32) * mask[i, j].astype(jnp.float32)
            live[rows, columns] = piece.astype(jnp.bfloat16)
            sums = sums + piece
        degree = jnp.sum(sums, axis=1, keepdims=True)
        inverse[rows, :] = jnp.broadcast_to(1.0 / jnp.sqrt(degree), (TILE, TILE))
        total[rows, :] = jnp.zeros((TILE, hidden), jnp.float32)

    bias_row = bias[...].reshape(1, hidden)

    def project(k):
        for peer in peers:
            arrival(k, peer).wait_recv()
        both = lax.dot_general(
            own[k], weights[...], (((0,), (0,)), ((), ())), preferred_element_type=jnp.float32
        )
        rows = pl.ds(pl.multiple_of(k * CHUNK, CHUNK), CHUNK)
        self_bias[rows, :] = both[:, :hidden] + bias_row
        projected[rows, :] = both[:, hidden:].astype(jnp.bfloat16)

    def sent(k):
        for peer in peers:
            arrival(k, peer).wait_send()

    def add_local(k):
        span = pl.ds(pl.multiple_of(k * CHUNK, CHUNK), CHUNK)
        panel = projected[span, :]

        @pl.loop(0, row_tiles)
        def _(i):
            rows = pl.ds(pl.multiple_of(i * TILE, TILE), TILE)
            total[rows, :] += jnp.dot(live[rows, span], panel, preferred_element_type=jnp.float32)

    def halo_copy(slot, peer):
        return pltpu.make_async_remote_copy(
            src_ref=projected.at[pl.ds(0, halo_len)],
            dst_ref=halo.at[pl.ds(slot * halo_len, halo_len)],
            send_sem=halo_send.at[slot],
            recv_sem=halo_recv.at[slot],
            device_id={"blk": peer},
            device_id_type=MESH,
        )

    @pl.loop(0, halo_chunks)
    def _(k):
        project(k)

    for slot, peer in enumerate(block_peers):
        halo_copy(slot, peer).start()

    @pl.loop(0, halo_chunks)
    def _(k):
        add_local(k)
        sent(k)

    for slot, peer in enumerate(block_peers):
        halo_copy(slot, peer).wait()

    @pl.loop(0, row_tiles)
    def _(i):
        rows = pl.ds(pl.multiple_of(i * TILE, TILE), TILE)
        total[rows, :] += jnp.dot(
            live[rows, pl.ds(nodes, remote)], halo[...], preferred_element_type=jnp.float32
        )

    @pl.loop(halo_chunks, chunks - 1)
    def _(k):
        project(k)
        add_local(k)
        sent(k)

    last = chunks - 1
    span = pl.ds(last * CHUNK, CHUNK)
    group = parts // 2
    near = (me // group) * group
    far = group - near

    def half(first):
        rows = pl.ds(pl.multiple_of(first * width, width), group * width)
        return lax.dot_general(
            own[last, rows], weights[rows, :], (((0,), (0,)), ((), ())),
            preferred_element_type=jnp.float32,
        )

    for d in range(1, group):
        arrival(last, near + lax.rem(me - near + d, group)).wait_recv()
    both = half(near)
    for d in range(group):
        arrival(last, far + d).wait_recv()
    both = both + half(far)
    self_bias[span, :] = both[:, :hidden] + bias_row
    panel = both[:, hidden:].astype(jnp.bfloat16)

    @pl.loop(0, row_tiles)
    def _(i):
        rows = pl.ds(pl.multiple_of(i * TILE, TILE), TILE)
        summed = total[rows, :] + jnp.dot(
            live[rows, span], panel, preferred_element_type=jnp.float32
        )
        scale = jnp.concatenate([inverse[rows, :]] * (hidden // TILE), axis=1)
        out[rows, :] = jnp.maximum(self_bias[rows, :] + summed * scale, 0.0).astype(jnp.bfloat16)

    sent(last)


def shards(features, adj_local, adj_remote, tile_mask, w_self, w_neigh, out_bias):
    parts = lax.axis_size("feat")
    blocks = lax.axis_size("blk")
    width, _, nodes = features.shape
    hidden = w_self.shape[1]
    remote = adj_remote.shape[1]
    chunks = nodes // CHUNK
    bf16, f32 = jnp.bfloat16, jnp.float32
    hbm = pl.BlockSpec(memory_space=pltpu.HBM)
    return pl.pallas_call(
        functools.partial(layer_kernel, parts, blocks),
        out_shape=pltpu.VMEM((nodes, hidden), bf16),
        in_specs=[hbm] * 7,
        out_specs=pl.BlockSpec(memory_space=pltpu.VMEM),
        scratch_shapes=[
            pltpu.VMEM((chunks, width, parts, CHUNK), bf16),
            pltpu.VMEM((CHUNK // TILE, width * parts, TILE), f32),
            pltpu.VMEM((chunks, parts, width, CHUNK), bf16),
            pltpu.VMEM((chunks, parts * width, CHUNK), bf16),
            pltpu.VMEM((nodes, nodes + remote), bf16),
            pltpu.SMEM(tile_mask.shape, jnp.int32),
            pltpu.VMEM((parts * width, 2 * hidden), bf16),
            pltpu.VMEM(out_bias.shape, f32),
            pltpu.VMEM((nodes, hidden), bf16),
            pltpu.VMEM((remote, hidden), bf16),
            pltpu.VMEM((nodes, hidden), f32),
            pltpu.VMEM((nodes, hidden), f32),
            pltpu.VMEM((nodes, TILE), f32),
            pltpu.SemaphoreType.DMA((chunks,)),
            pltpu.SemaphoreType.DMA((6,)),
            pltpu.SemaphoreType.DMA((chunks, parts)),
            pltpu.SemaphoreType.DMA((chunks, parts)),
            pltpu.SemaphoreType.DMA((blocks - 1,)),
            pltpu.SemaphoreType.DMA((blocks - 1,)),
        ],
        compiler_params=pltpu.CompilerParams(
            collective_id=0, has_side_effects=True, vmem_limit_bytes=62 * 1024 * 1024
        ),
    )(features, adj_local, adj_remote, tile_mask, w_self, w_neigh, out_bias)


def solution(mesh):
    placed = (
        P("feat", None, "blk"),
        P(("feat", "blk"), None),
        P(("feat", "blk"), None),
        P(("feat", "blk"), None),
        P(),
        P(),
        P(),
    )
    return jax.shard_map(
        shards, mesh=mesh, in_specs=placed, out_specs=P(("feat", "blk"), None), check_vma=False
    )
```
